32 devices in a mesh: ga: 4 (over y, core), band: 8 (over z, x).
Axes of the slice: x: 2, y: 2, z: 4, core: 2. Of those that a mesh axis runs over, the one named last changes fastest.
Arguments:
- coeffs: float32 [8, 4096, 128], P('band', 'ga'), may hold values from -6 to 6
- potential: bfloat16 [256, 256, 256], P('ga'), may hold values from -2 to 1
- stick_cells: int32 [4096], replicated, may hold values from 0 to 65535, as said below
- block: bfloat16 [64, 524288], P('band', 'ga'), may hold values from -6 to 6
- rotation: bfloat16 [64, 8], P('band'), may hold values from -2 to 2
Outputs:
- h_coeffs: float32 [8, 4096, 128], P('band', 'ga')
- rotated: bfloat16 [64, 524288], P('band', 'ga')
The draws below stay inside these ranges and needn't reach their ends.
Inputs may be any that keep to these rules, and one draw needn't show every extreme that they name: `stick_cells`: distinct cells: the 4096 cells of the 256 x 256 plane nearest to zero frequency in wrapped distance, ties at the rim broken at random, listed in random order.
All inputs are finite; a program needn't handle non-finite values.
Results may differ from the reference program's by a relative error of at most 0.0039.
Values may be sent and summed in bfloat16 or wider, within the bound.
A program may use at most 128 MiB of HBM per device.

```python
import math
import jax
import jax.numpy as jnp
from jax import lax

N1 = 256
N2 = 256
N3 = 256
ZC = 128
COLS = 4096
NG = 524288
HB = 8
RB = 64


def draw_stick_cells(key, part):
    key_rank = jax.random.fold_in(key, 11)
    key_order = jax.random.fold_in(key, 23)
    cell_ids = jnp.arange(N1 * N2, dtype=jnp.int32)
    pos_x = cell_ids // N2
    pos_y = cell_ids % N2
    wrap_x = jnp.where(2 * pos_x <= N1, pos_x, pos_x - N1)
    wrap_y = jnp.where(2 * pos_y <= N2, pos_y, pos_y - N2)
    radius_sq = wrap_x * wrap_x + wrap_y * wrap_y
    noise = jax.random.randint(key_rank, (N1 * N2,), 0, 4096, dtype=jnp.int32)
    scores = radius_sq * 4096 + noise
    chosen = jnp.argsort(scores, stable=True)[:COLS].astype(jnp.int32)
    order = jax.random.permutation(key_order, COLS)
    return chosen[order].astype(jnp.int32)


def steps_of(stream_key, extent, shards, low, high):
    gain, own = 1.0, jax.random.fold_in(stream_key, 6)
    for dim, shards_of in shards:
        steps = jnp.exp(jax.random.uniform(jax.random.fold_in(own, dim), (shards_of,), jnp.float32, low / len(shards), high / len(shards)))
        gain = gain * jnp.repeat(steps, extent[dim] // shards_of).reshape([-1 if axis == dim else 1 for axis in range(len(extent))])
    return gain


def scatter_about(rng, dims, spread, limit, split=(), kind=jnp.bfloat16):
    loudness = steps_of(rng, dims, split, -0.22, 0.18) if split else 1.0
    values = jax.random.normal(rng, dims, jnp.float32) * spread * loudness
    return jnp.minimum(jnp.maximum(values, -limit), limit).astype(kind)


def setup_inputs(seed: int = 0) -> dict:
    keys = jax.random.split(jax.random.key(seed), 6)
    coeffs = scatter_about(keys[0], (HB, COLS, ZC), 1.0, 6.0, ((0, 8), (1, 4)), jnp.float32)
    potential = jnp.clip(-2.0 + 3.0 * jax.random.uniform(keys[1], (N3, N1, N2), jnp.float32) ** steps_of(keys[1], (N3, N1, N2), ((0, 4),), -0.2, 0.2), -2.0, 1.0).astype(jnp.bfloat16)
    stick_cells = draw_stick_cells(jax.random.fold_in(keys[5], 71), 0)
    block = scatter_about(keys[3], (RB, NG), 1.0, 6.0, ((0, 8), (1, 4)))
    rotation = scatter_about(keys[4], (RB, HB), HB ** -0.5, 2.0, ((0, 8),))
    return dict(coeffs=coeffs, potential=potential, stick_cells=stick_cells, block=block, rotation=rotation)


def hartley(count):
    index_row = jnp.arange(count, dtype=jnp.int32)
    product = index_row[:, None] * index_row[None, :] % count
    angles = product.astype(jnp.float32) * (2.0 * math.pi / count)
    return (jnp.cos(angles) + jnp.sin(angles)) / math.sqrt(count)

def slot_index(slots, size_z):
    index_row = jnp.arange(slots, dtype=jnp.int32)
    return jnp.where(2 * index_row < slots, index_row, index_row + size_z - slots).astype(jnp.int32)

def signed_freq(values, count):
    return jnp.where(2 * values <= count, values, values - count).astype(jnp.float32)

def kinetic_table(cells, size_x, size_y, size_z, slot_ids):
    freq_x = signed_freq(cells // size_y, size_x)
    freq_y = signed_freq(cells % size_y, size_y)
    freq_z = signed_freq(slot_ids, size_z)
    plane_part = 0.5 * ((2.0 * math.pi / size_x) ** 2 * freq_x * freq_x + (2.0 * math.pi / size_y) ** 2 * freq_y * freq_y)
    line_part = 0.5 * (2.0 * math.pi / size_z) ** 2 * freq_z * freq_z
    return plane_part[:, None] + line_part[None, :]

def reference(coeffs, potential, stick_cells, block, rotation):
    highest = lax.Precision.HIGHEST
    table_x = hartley(N1)
    table_y = hartley(N2)
    slot_ids = slot_index(ZC, N3)
    table_z = hartley(N3)[:, slot_ids]
    kinetic = kinetic_table(stick_cells, N1, N2, N3, slot_ids)
    pot_field = potential.astype(jnp.float32)

    def apply_one(band_coeffs):
        columns = jnp.einsum('sk,zk->zs', band_coeffs, table_z, precision=highest)
        grid = jnp.zeros((N3, N1 * N2), jnp.float32).at[:, stick_cells].set(columns)
        grid = grid.reshape(N3, N1, N2)
        field = jnp.einsum('zxy,vy->zxv', grid, table_y, precision=highest)
        field = jnp.einsum('zxy,ux->zuy', field, table_x, precision=highest)
        product = field * pot_field
        back = jnp.einsum('zxy,vy->zxv', product, table_y, precision=highest)
        back = jnp.einsum('zxy,ux->zuy', back, table_x, precision=highest)
        picked = back.reshape(N3, N1 * N2)[:, stick_cells]
        return jnp.einsum('zs,zk->sk', picked, table_z, precision=highest) + kinetic * band_coeffs
    h_coeffs = lax.map(apply_one, coeffs)
    panel = h_coeffs.reshape(HB, NG).astype(jnp.bfloat16)
    rotated = (block.astype(jnp.float32) + jnp.dot(rotation, panel, preferred_element_type=jnp.float32)).astype(jnp.bfloat16)
    return (h_coeffs, rotated)
```

```python
import functools
import math

import jax
import jax.numpy as jnp
import numpy as np
from jax import lax
from jax.experimental import pallas as pl
from jax.experimental.pallas import tpu as pltpu
from jax.sharding import PartitionSpec as P

BF16 = jnp.bfloat16
F32 = jnp.float32
LEVEL = -0.5


def hartley(count):
    index_row = np.arange(count, dtype=np.int64)
    angles = (index_row[:, None] * index_row[None, :] % count) * (2.0 * math.pi / count)
    return (np.cos(angles) + np.sin(angles)) / math.sqrt(count)


def slot_index(slots, size_z):
    index_row = np.arange(slots)
    return np.where(2 * index_row < slots, index_row, index_row + size_z - slots)


def signed_np(values, count):
    return np.where(2 * values <= count, values, values - count)


def reach(cols, size_x, size_y):
    fx = signed_np(np.arange(size_x), size_x)
    fy = signed_np(np.arange(size_y), size_y)
    radius_sq = np.sort((fx[:, None] ** 2 + fy[None, :] ** 2).reshape(-1))
    return math.isqrt(int(radius_sq[cols - 1]))


def window(radius, size, step):
    return min(size, -(-(2 * radius + 1) // step) * step)


def signed_freq(values, count):
    return jnp.where(2 * values <= count, values, values - count)


def loop(count):
    return lambda step_fn: lax.fori_loop(0, count, step_fn, 0)


def plane_kernel(
    xw, yw, rows_ref, spread_ref, pot_ref, sy_ref, syt_ref, sx_ref, sxt_ref, out_ref, grid_ref, line_ref
):
    planes = pot_ref.shape[0]
    cols = spread_ref.shape[0]
    grid_ref[...] = jnp.zeros_like(grid_ref)

    @loop(cols // 32)
    def _(step, carry):
        base = pl.multiple_of(step * 32, 32)
        for i in range(32):
            grid_ref[pl.ds(rows_ref[base + i], 1), :] = spread_ref[pl.ds(base + i, 1), :]
        return carry

    for slot in range(xw):
        chunk = jnp.transpose(grid_ref[slot * yw : (slot + 1) * yw, :])
        for half in range(yw // 128):
            line_ref[half, pl.ds(slot, planes, stride=xw), :] = chunk[:planes, half * 128 : (half + 1) * 128]

    @loop(planes // 2)
    def _(step, carry):
        for i in range(2):
            plane = step * 2 + i
            at = pl.ds(pl.multiple_of(plane * xw, xw), xw)
            parts = [line_ref[half, at, :].astype(BF16) for half in range(yw // 128)]
            part = parts[0] if len(parts) == 1 else jnp.concatenate(parts, axis=1)
            lines = jnp.dot(part, sy_ref[...], preferred_element_type=F32).astype(BF16)
            field = jnp.dot(sx_ref[...], lines, preferred_element_type=F32)
            product = (field * (pot_ref[plane].astype(F32) - LEVEL)).astype(BF16)
            lines = jnp.dot(sxt_ref[...], product, preferred_element_type=F32).astype(BF16)
            back = jnp.dot(lines, syt_ref[...], preferred_element_type=F32)
            for half in range(yw // 128):
                line_ref[half, at, :] = back[:, half * 128 : (half + 1) * 128]
        return carry

    for slot in range(xw):
        parts = [line_ref[half, pl.ds(slot, planes, stride=xw), :] for half in range(yw // 128)]
        chunk = parts[0] if len(parts) == 1 else jnp.concatenate(parts, axis=1)
        if planes < 128:
            chunk = jnp.concatenate([chunk, jnp.zeros((128 - planes, yw), F32)], axis=0)
        grid_ref[slot * yw : (slot + 1) * yw, :] = jnp.transpose(chunk)

    @loop(cols // 32)
    def _(step, carry):
        base = pl.multiple_of(step * 32, 32)
        for i in range(32):
            out_ref[pl.ds(base + i, 1), :] = grid_ref[pl.ds(rows_ref[base + i], 1), :]
        return carry


def apply_planes(rows, spread, potential, xw, yw):
    planes, size_x, size_y = potential.shape
    cols = spread.shape[0]
    table_x = hartley(size_x)[:, (np.arange(xw) - xw // 2) % size_x]
    table_y = hartley(size_y)[:, (np.arange(yw) - yw // 2) % size_y]
    vmem = pl.BlockSpec(memory_space=pltpu.VMEM)
    cast = lambda a: jnp.asarray(a, BF16)
    return pl.pallas_call(
        functools.partial(plane_kernel, xw, yw),
        out_shape=jax.ShapeDtypeStruct((cols, 128), F32),
        in_specs=[pl.BlockSpec(memory_space=pltpu.SMEM)] + [vmem] * 6,
        out_specs=vmem,
        scratch_shapes=[
            pltpu.VMEM((xw * yw, 128), F32),
            pltpu.VMEM((yw // 128, planes * xw, 128), F32),
        ],
        compiler_params=pltpu.CompilerParams(vmem_limit_bytes=56 * 2**20),
    )(rows, spread, potential, cast(table_y.T), cast(table_y), cast(table_x), cast(table_x.T))


def body(coeffs, potential, stick_cells, block, rotation):
    col_count, slots = coeffs.shape[1:]
    planes, size_x, size_y = potential.shape
    groups = lax.axis_size("ga")
    cols = stick_cells.shape[0]
    size_z = planes * groups
    radius = reach(cols, size_x, size_y)
    xw = window(radius, size_x, 16)
    yw = window(radius, size_y, 128)
    slot_ids = slot_index(slots, size_z)
    table_z = hartley(size_z)[:, slot_ids]
    freq_x = signed_freq(stick_cells // size_y, size_x)
    freq_y = signed_freq(stick_cells % size_y, size_y)
    rows = (freq_x + xw // 2) * yw + freq_y + yw // 2

    mine = lax.axis_index("ga") * col_count
    local_x = lax.dynamic_slice_in_dim(freq_x, mine, col_count).astype(F32)
    local_y = lax.dynamic_slice_in_dim(freq_y, mine, col_count).astype(F32)
    plane_part = 0.5 * (
        (2.0 * math.pi / size_x) ** 2 * local_x * local_x
        + (2.0 * math.pi / size_y) ** 2 * local_y * local_y
    )
    freq_z = signed_np(slot_ids, size_z)
    line_part = jnp.asarray(0.5 * (2.0 * math.pi / size_z) ** 2 * freq_z * freq_z, F32)
    kinetic = plane_part[:, None] + line_part[None, :]

    table_f = jnp.asarray(table_z.reshape(groups, planes, slots), F32)
    table_b = jnp.asarray(table_z.reshape(groups, planes, slots), F32)
    high = lax.Precision.HIGH
    sent = jnp.einsum("sk,gzk->gsz", coeffs[0], table_f, precision=high).astype(BF16)
    spread = lax.all_to_all(sent, "ga", split_axis=0, concat_axis=0, tiled=True)
    spread = spread.reshape(cols, planes).astype(F32)
    spread = jnp.pad(spread, ((0, 0), (0, 128 - planes)))
    picked = apply_planes(rows, spread, potential, xw, yw)
    picked = picked[:, :planes].astype(BF16).reshape(groups, col_count, planes)
    returned = lax.all_to_all(picked, "ga", split_axis=0, concat_axis=0, tiled=True)
    results = (
        jnp.einsum("gsz,gzk->sk", returned.astype(F32), table_b, precision=high) + (kinetic + LEVEL) * coeffs[0]
    )
    panel = results.reshape(1, col_count * slots).astype(BF16)
    summed = jnp.dot(
        rotation,
        lax.all_gather(panel, "band", axis=0, tiled=True),
        preferred_element_type=F32,
    )
    rotated = (block.astype(F32) + summed).astype(BF16)
    return (results[None], rotated)


def solution(mesh):
    return jax.shard_map(
        body,
        mesh=mesh,
        in_specs=(
            P("band", "ga", None),
            P("ga", None, None),
            P(),
            P("band", "ga"),
            P("band", None),
        ),
        out_specs=(P("band", "ga", None), P("band", "ga")),
        check_vma=False,
    )
```

```python
import functools
import math

import jax
import jax.numpy as jnp
import numpy as np
from jax import lax
from jax.experimental import pallas as pl
from jax.experimental.pallas import tpu as pltpu
from jax.sharding import PartitionSpec as P

BF16 = jnp.bfloat16
F32 = jnp.float32
LEVEL = -0.5


def hartley(count):
    index_row = np.arange(count, dtype=np.int64)
    angles = (index_row[:, None] * index_row[None, :] % count) * (2.0 * math.pi / count)
    return (np.cos(angles) + np.sin(angles)) / math.sqrt(count)


def slot_index(slots, size_z):
    index_row = np.arange(slots)
    return np.where(2 * index_row < slots, index_row, index_row + size_z - slots)


def signed_np(values, count):
    return np.where(2 * values <= count, values, values - count)


def reach(cols, size_x, size_y):
    fx = signed_np(np.arange(size_x), size_x)
    fy = signed_np(np.arange(size_y), size_y)
    radius_sq = np.sort((fx[:, None] ** 2 + fy[None, :] ** 2).reshape(-1))
    return math.isqrt(int(radius_sq[cols - 1]))


def window(radius, size, step):
    return min(size, -(-(2 * radius + 1) // step) * step)


def signed_freq(values, count):
    return jnp.where(2 * values <= count, values, values - count)


def loop(count):
    return lambda step_fn: lax.fori_loop(0, count, step_fn, 0)


def plane_kernel(
    xw, yw, rows_ref, spread_ref, pot_ref, sy_ref, syt_ref, sx_ref, sxt_ref, out_ref, cols_ref, grid_ref, line_ref
):
    planes = pot_ref.shape[0]
    cols = spread_ref.shape[0]
    grid_ref[...] = jnp.zeros_like(grid_ref)
    cols_ref[:, :planes] = spread_ref[...].astype(F32)

    @loop(cols // 32)
    def _(step, carry):
        base = pl.multiple_of(step * 32, 32)
        for i in range(32):
            grid_ref[pl.ds(rows_ref[base + i], 1), :] = cols_ref[pl.ds(base + i, 1), :]
        return carry

    for slot in range(xw):
        chunk = jnp.transpose(grid_ref[slot * yw : (slot + 1) * yw, :])
        for half in range(yw // 128):
            line_ref[half, pl.ds(slot, planes, stride=xw), :] = chunk[:planes, half * 128 : (half + 1) * 128]

    @loop(planes // 2)
    def _(step, carry):
        for i in range(2):
            plane = step * 2 + i
            at = pl.ds(pl.multiple_of(plane * xw, xw), xw)
            parts = [line_ref[half, at, :].astype(BF16) for half in range(yw // 128)]
            part = parts[0] if len(parts) == 1 else jnp.concatenate(parts, axis=1)
            lines = jnp.dot(part, sy_ref[...], preferred_element_type=F32).astype(BF16)
            field = jnp.dot(sx_ref[...], lines, preferred_element_type=F32)
            product = (field * (pot_ref[plane].astype(F32) - LEVEL)).astype(BF16)
            lines = jnp.dot(sxt_ref[...], product, preferred_element_type=F32).astype(BF16)
            back = jnp.dot(lines, syt_ref[...], preferred_element_type=F32)
            for half in range(yw // 128):
                line_ref[half, at, :] = back[:, half * 128 : (half + 1) * 128]
        return carry

    for slot in range(xw):
        parts = [line_ref[half, pl.ds(slot, planes, stride=xw), :] for half in range(yw // 128)]
        chunk = parts[0] if len(parts) == 1 else jnp.concatenate(parts, axis=1)
        if planes < 128:
            chunk = jnp.concatenate([chunk, jnp.zeros((128 - planes, yw), F32)], axis=0)
        grid_ref[slot * yw : (slot + 1) * yw, :] = jnp.transpose(chunk)

    @loop(cols // 32)
    def _(step, carry):
        base = pl.multiple_of(step * 32, 32)
        for i in range(32):
            cols_ref[pl.ds(base + i, 1), :] = grid_ref[pl.ds(rows_ref[base + i], 1), :]
        return carry

    out_ref[...] = cols_ref[:, :planes].astype(BF16)


def apply_planes(rows, spread, potential, xw, yw):
    planes, size_x, size_y = potential.shape
    cols = spread.shape[0]
    table_x = hartley(size_x)[:, (np.arange(xw) - xw // 2) % size_x]
    table_y = hartley(size_y)[:, (np.arange(yw) - yw // 2) % size_y]
    vmem = pl.BlockSpec(memory_space=pltpu.VMEM)
    cast = lambda a: jnp.asarray(a, BF16)
    return pl.pallas_call(
        functools.partial(plane_kernel, xw, yw),
        out_shape=jax.ShapeDtypeStruct((cols, planes), BF16),
        in_specs=[pl.BlockSpec(memory_space=pltpu.SMEM)] + [vmem] * 6,
        out_specs=vmem,
        scratch_shapes=[
            pltpu.VMEM((cols, 128), F32),
            pltpu.VMEM((xw * yw, 128), F32),
            pltpu.VMEM((yw // 128, planes * xw, 128), F32),
        ],
        compiler_params=pltpu.CompilerParams(vmem_limit_bytes=56 * 2**20),
    )(rows, spread, potential, cast(table_y.T), cast(table_y), cast(table_x), cast(table_x.T))


def gather_kernel(
    depth, width, pieces, own_ref, out_ref, own_sem, line_send, line_recv, cross_send, cross_recv
):
    band = lax.axis_index("band")
    z = band // width
    x = band % width
    rows = own_ref.shape[0] // pieces
    ways = (1, -1)

    def inside(at):
        return jnp.logical_and(at >= 0, at < depth)

    def source(d, slot, cut):
        return own_ref.at[cut, :] if d == 0 else out_ref.at[slot, cut, :]

    def line_copy(way, d, piece):
        cut = pl.ds(piece * rows, rows)
        slot = (z - ways[way] * d) * width + x
        return pltpu.make_async_remote_copy(
            src_ref=source(d, slot, cut),
            dst_ref=out_ref.at[slot, cut, :],
            send_sem=line_send.at[way, d, piece],
            recv_sem=line_recv.at[way, d, piece],
            device_id={"band": (z + ways[way]) * width + x},
            device_id_type=pl.DeviceIdType.MESH,
        )

    def cross_copy(hop, way, d, piece):
        cut = pl.ds(piece * rows, rows)
        slot = (z - ways[way] * d) * width + x
        return pltpu.make_async_remote_copy(
            src_ref=source(d, slot, cut),
            dst_ref=out_ref.at[slot, cut, :],
            send_sem=cross_send.at[hop - 1, way, d, piece],
            recv_sem=cross_recv.at[hop - 1, way, d, piece],
            device_id={"band": z * width + (x + hop) % width},
            device_id_type=pl.DeviceIdType.MESH,
        )

    def line_arrival(way, d, piece):
        cut = pl.ds(piece * rows, rows)
        slot = (z - ways[way] * d) * width + x
        return pltpu.make_async_copy(
            out_ref.at[slot, cut, :], out_ref.at[slot, cut, :], line_recv.at[way, d - 1, piece]
        )

    def cross_arrival(hop, way, d, piece):
        cut = pl.ds(piece * rows, rows)
        slot = (z - ways[way] * d) * width + (x + width - hop) % width
        return pltpu.make_async_copy(
            out_ref.at[slot, cut, :], out_ref.at[slot, cut, :], cross_recv.at[hop - 1, way, d, piece]
        )

    barrier = pltpu.get_barrier_semaphore()
    for way in ways:

        @pl.when(inside(z + way))
        def _(way=way):
            pl.semaphore_signal(
                barrier,
                inc=1,
                device_id={"band": (z + way) * width + x},
                device_id_type=pl.DeviceIdType.MESH,
            )

    for hop in range(1, width):
        pl.semaphore_signal(
            barrier,
            inc=1,
            device_id={"band": z * width + (x + hop) % width},
            device_id_type=pl.DeviceIdType.MESH,
        )
    beside = jnp.where(z > 0, 1, 0) + jnp.where(z < depth - 1, 1, 0)
    pl.semaphore_wait(barrier, beside + width - 1)

    own = pltpu.make_async_copy(own_ref, out_ref.at[band], own_sem)
    own.start()

    for d in range(depth):
        for piece in range(pieces):
            for way in range(2):

                @pl.when(inside(z - ways[way] * d))
                def _(way=way):
                    if d > 0:
                        line_arrival(way, d, piece).wait()

                    if d < depth - 1:

                        @pl.when(inside(z + ways[way]))
                        def _():
                            line_copy(way, d, piece).start()

                    if d > 0 or way == 0:
                        for hop in range(1, width):
                            cross_copy(hop, way, d, piece).start()

    own.wait()
    for d in range(depth):
        for piece in range(pieces):
            for way in range(2):

                @pl.when(inside(z - ways[way] * d))
                def _(way=way):
                    if d < depth - 1:

                        @pl.when(inside(z + ways[way]))
                        def _():
                            line_copy(way, d, piece).wait_send()

                    if d > 0 or way == 0:
                        for hop in range(1, width):
                            cross_copy(hop, way, d, piece).wait_send()
                            cross_arrival(hop, way, d, piece).wait()


def gather_panel(own, bands):
    width = bands // 4 if bands % 4 == 0 and bands > 4 else 1
    depth = bands // width
    pieces = 2
    line = pltpu.SemaphoreType.DMA((2, depth, pieces))
    cross = pltpu.SemaphoreType.DMA((max(width - 1, 1), 2, depth, pieces))
    anywhere = pl.BlockSpec(memory_space=pl.ANY)
    return pl.pallas_call(
        functools.partial(gather_kernel, depth, width, pieces),
        out_shape=jax.ShapeDtypeStruct((bands,) + own.shape, own.dtype),
        in_specs=[anywhere],
        out_specs=anywhere,
        scratch_shapes=[pltpu.SemaphoreType.DMA, line, line, cross, cross],
        compiler_params=pltpu.CompilerParams(collective_id=0, has_side_effects=True),
    )(own)


def body(coeffs, potential, stick_cells, block, rotation):
    col_count, slots = coeffs.shape[1:]
    planes, size_x, size_y = potential.shape
    groups = lax.axis_size("ga")
    cols = stick_cells.shape[0]
    size_z = planes * groups
    radius = reach(cols, size_x, size_y)
    xw = window(radius, size_x, 16)
    yw = window(radius, size_y, 128)
    slot_ids = slot_index(slots, size_z)
    table_z = hartley(size_z)[:, slot_ids]
    freq_x = signed_freq(stick_cells // size_y, size_x)
    freq_y = signed_freq(stick_cells % size_y, size_y)
    rows = (freq_x + xw // 2) * yw + freq_y + yw // 2

    mine = lax.axis_index("ga") * col_count
    local_x = lax.dynamic_slice_in_dim(freq_x, mine, col_count).astype(F32)
    local_y = lax.dynamic_slice_in_dim(freq_y, mine, col_count).astype(F32)
    plane_part = 0.5 * (
        (2.0 * math.pi / size_x) ** 2 * local_x * local_x
        + (2.0 * math.pi / size_y) ** 2 * local_y * local_y
    )
    freq_z = signed_np(slot_ids, size_z)
    line_part = jnp.asarray(0.5 * (2.0 * math.pi / size_z) ** 2 * freq_z * freq_z, F32)
    kinetic = plane_part[:, None] + line_part[None, :]

    table_f = jnp.asarray(table_z.reshape(groups, planes, slots), F32)
    table_b = jnp.asarray(table_z.reshape(groups, planes, slots), F32)
    high = lax.Precision.HIGH
    sent = jnp.einsum("sk,gzk->gsz", coeffs[0], table_f, precision=high).astype(BF16)
    spread = lax.all_to_all(sent, "ga", split_axis=0, concat_axis=0, tiled=True)
    spread = spread.reshape(cols, planes)
    picked = apply_planes(rows, spread, potential, xw, yw)
    picked = picked.reshape(groups, col_count, planes)
    returned = lax.all_to_all(picked, "ga", split_axis=0, concat_axis=0, tiled=True)
    results = (
        jnp.einsum("gsz,gzk->sk", returned.astype(F32), table_b, precision=high) + (kinetic + LEVEL) * coeffs[0]
    )
    panel = gather_panel(results.astype(BF16), lax.axis_size("band"))
    summed = jnp.dot(
        rotation,
        panel.reshape(panel.shape[0], col_count * slots),
        preferred_element_type=F32,
    )
    rotated = (block.astype(F32) + summed).astype(BF16)
    return (results[None], rotated)


def solution(mesh):
    return jax.shard_map(
        body,
        mesh=mesh,
        in_specs=(
            P("band", "ga", None),
            P("ga", None, None),
            P(),
            P("band", "ga"),
            P("band", None),
        ),
        out_specs=(P("band", "ga", None), P("band", "ga")),
        check_vma=False,
    )
```

```python
import functools
import math

import jax
import jax.numpy as jnp
import numpy as np
from jax import lax
from jax.experimental import pallas as pl
from jax.experimental.pallas import tpu as pltpu
from jax.sharding import PartitionSpec as P

BF16 = jnp.bfloat16
F32 = jnp.float32
LEVEL = -0.5
BATCH = 8


def hartley(count):
    index_row = np.arange(count, dtype=np.int64)
    angles = (index_row[:, None] * index_row[None, :] % count) * (2.0 * math.pi / count)
    return (np.cos(angles) + np.sin(angles)) / math.sqrt(count)


def slot_index(slots, size_z):
    index_row = np.arange(slots)
    return np.where(2 * index_row < slots, index_row, index_row + size_z - slots)


def signed_np(values, count):
    return np.where(2 * values <= count, values, values - count)


def reach(cols, size_x, size_y):
    fx = signed_np(np.arange(size_x), size_x)
    fy = signed_np(np.arange(size_y), size_y)
    radius_sq = np.sort((fx[:, None] ** 2 + fy[None, :] ** 2).reshape(-1))
    return math.isqrt(int(radius_sq[cols - 1]))


def window(radius, size, step):
    return min(size, -(-(2 * radius + 1) // step) * step)


def signed_freq(values, count):
    return jnp.where(2 * values <= count, values, values - count)


def loop(count):
    return lambda step_fn: lax.fori_loop(0, count, step_fn, 0)


def plane_kernel(
    xw, yw, rows_ref, spread_ref, pot_ref, sy_ref, syt_ref, sx_ref, sxt_ref, out_ref, cols_ref, grid_ref, line_ref
):
    planes = pot_ref.shape[0]
    cols = spread_ref.shape[0]
    grid_ref[...] = jnp.zeros_like(grid_ref)
    cols_ref[:, :planes] = spread_ref[...].astype(F32)

    @loop(cols // 32)
    def _(step, carry):
        base = pl.multiple_of(step * 32, 32)
        for i in range(32):
            grid_ref[pl.ds(rows_ref[base + i], 1), :] = cols_ref[pl.ds(base + i, 1), :]
        return carry

    for slot in range(xw):
        chunk = jnp.transpose(grid_ref[slot * yw : (slot + 1) * yw, :])
        for half in range(yw // 128):
            line_ref[half, pl.ds(slot, planes, stride=xw), :] = chunk[:planes, half * 128 : (half + 1) * 128]

    @loop(planes // BATCH)
    def _(step, carry):
        ats = [pl.ds(pl.multiple_of((step * BATCH + i) * xw, xw), xw) for i in range(BATCH)]
        halves = range(yw // 128)
        def join(parts):
            return parts[0] if len(parts) == 1 else jnp.concatenate(parts, axis=1)
        part = jnp.concatenate([join([line_ref[h, at, :].astype(BF16) for h in halves]) for at in ats], axis=0)
        lines = jnp.dot(part, sy_ref[...], preferred_element_type=F32).astype(BF16)
        low = []
        for i in range(BATCH):
            field = jnp.dot(sx_ref[...], lines[i * xw : (i + 1) * xw], preferred_element_type=F32)
            product = (field * (pot_ref[step * BATCH + i].astype(F32) - LEVEL)).astype(BF16)
            low.append(jnp.dot(sxt_ref[...], product, preferred_element_type=F32).astype(BF16))
        back = jnp.dot(jnp.concatenate(low, axis=0), syt_ref[...], preferred_element_type=F32)
        for i, at in enumerate(ats):
            for h in halves:
                line_ref[h, at, :] = back[i * xw : (i + 1) * xw, h * 128 : (h + 1) * 128]
        return carry

    for slot in range(xw):
        parts = [line_ref[half, pl.ds(slot, planes, stride=xw), :] for half in range(yw // 128)]
        chunk = parts[0] if len(parts) == 1 else jnp.concatenate(parts, axis=1)
        if planes < 128:
            chunk = jnp.concatenate([chunk, jnp.zeros((128 - planes, yw), F32)], axis=0)
        grid_ref[slot * yw : (slot + 1) * yw, :] = jnp.transpose(chunk)

    @loop(cols // 32)
    def _(step, carry):
        base = pl.multiple_of(step * 32, 32)
        for i in range(32):
            cols_ref[pl.ds(base + i, 1), :] = grid_ref[pl.ds(rows_ref[base + i], 1), :]
        return carry

    out_ref[...] = cols_ref[:, :planes].astype(BF16)


def apply_planes(rows, spread, potential, xw, yw):
    planes, size_x, size_y = potential.shape
    cols = spread.shape[0]
    table_x = hartley(size_x)[:, (np.arange(xw) - xw // 2) % size_x]
    table_y = hartley(size_y)[:, (np.arange(yw) - yw // 2) % size_y]
    vmem = pl.BlockSpec(memory_space=pltpu.VMEM)
    cast = lambda a: jnp.asarray(a, BF16)
    return pl.pallas_call(
        functools.partial(plane_kernel, xw, yw),
        out_shape=jax.ShapeDtypeStruct((cols, planes), BF16),
        in_specs=[pl.BlockSpec(memory_space=pltpu.SMEM)] + [vmem] * 6,
        out_specs=vmem,
        scratch_shapes=[
            pltpu.VMEM((cols, 128), F32),
            pltpu.VMEM((xw * yw, 128), F32),
            pltpu.VMEM((yw // 128, planes * xw, 128), F32),
        ],
        compiler_params=pltpu.CompilerParams(vmem_limit_bytes=56 * 2**20),
    )(rows, spread, potential, cast(table_y.T), cast(table_y), cast(table_x), cast(table_x.T))


def gather_kernel(
    depth, width, pieces, own_ref, out_ref, own_sem, line_send, line_recv, cross_send, cross_recv
):
    band = lax.axis_index("band")
    z = band // width
    x = band % width
    rows = own_ref.shape[0] // pieces
    ways = (1, -1)

    def inside(at):
        return jnp.logical_and(at >= 0, at < depth)

    def source(d, slot, cut):
        return own_ref.at[cut, :] if d == 0 else out_ref.at[slot, cut, :]

    def line_copy(way, d, piece):
        cut = pl.ds(piece * rows, rows)
        slot = (z - ways[way] * d) * width + x
        return pltpu.make_async_remote_copy(
            src_ref=source(d, slot, cut),
            dst_ref=out_ref.at[slot, cut, :],
            send_sem=line_send.at[way, d, piece],
            recv_sem=line_recv.at[way, d, piece],
            device_id={"band": (z + ways[way]) * width + x},
            device_id_type=pl.DeviceIdType.MESH,
        )

    def cross_copy(hop, way, d, piece):
        cut = pl.ds(piece * rows, rows)
        slot = (z - ways[way] * d) * width + x
        return pltpu.make_async_remote_copy(
            src_ref=source(d, slot, cut),
            dst_ref=out_ref.at[slot, cut, :],
            send_sem=cross_send.at[hop - 1, way, d, piece],
            recv_sem=cross_recv.at[hop - 1, way, d, piece],
            device_id={"band": z * width + (x + hop) % width},
            device_id_type=pl.DeviceIdType.MESH,
        )

    def line_arrival(way, d, piece):
        cut = pl.ds(piece * rows, rows)
        slot = (z - ways[way] * d) * width + x
        return pltpu.make_async_copy(
            out_ref.at[slot, cut, :], out_ref.at[slot, cut, :], line_recv.at[way, d - 1, piece]
        )

    def cross_arrival(hop, way, d, piece):
        cut = pl.ds(piece * rows, rows)
        slot = (z - ways[way] * d) * width + (x + width - hop) % width
        return pltpu.make_async_copy(
            out_ref.at[slot, cut, :], out_ref.at[slot, cut, :], cross_recv.at[hop - 1, way, d, piece]
        )

    barrier = pltpu.get_barrier_semaphore()
    for way in ways:

        @pl.when(inside(z + way))
        def _(way=way):
            pl.semaphore_signal(
                barrier,
                inc=1,
                device_id={"band": (z + way) * width + x},
                device_id_type=pl.DeviceIdType.MESH,
            )

    for hop in range(1, width):
        pl.semaphore_signal(
            barrier,
            inc=1,
            device_id={"band": z * width + (x + hop) % width},
            device_id_type=pl.DeviceIdType.MESH,
        )
    beside = jnp.where(z > 0, 1, 0) + jnp.where(z < depth - 1, 1, 0)
    pl.semaphore_wait(barrier, beside + width - 1)

    own = pltpu.make_async_copy(own_ref, out_ref.at[band], own_sem)
    own.start()

    for d in range(depth):
        for piece in range(pieces):
            for way in range(2):

                @pl.when(inside(z - ways[way] * d))
                def _(way=way):
                    if d > 0:
                        line_arrival(way, d, piece).wait()

                    if d < depth - 1:

                        @pl.when(inside(z + ways[way]))
                        def _():
                            line_copy(way, d, piece).start()

                    if d > 0 or way == 0:
                        for hop in range(1, width):
                            cross_copy(hop, way, d, piece).start()

    own.wait()
    for d in range(depth):
        for piece in range(pieces):
            for way in range(2):

                @pl.when(inside(z - ways[way] * d))
                def _(way=way):
                    if d < depth - 1:

                        @pl.when(inside(z + ways[way]))
                        def _():
                            line_copy(way, d, piece).wait_send()

                    if d > 0 or way == 0:
                        for hop in range(1, width):
                            cross_copy(hop, way, d, piece).wait_send()
                            cross_arrival(hop, way, d, piece).wait()


def gather_panel(own, bands):
    width = bands // 4 if bands % 4 == 0 and bands > 4 else 1
    depth = bands // width
    pieces = 2
    line = pltpu.SemaphoreType.DMA((2, depth, pieces))
    cross = pltpu.SemaphoreType.DMA((max(width - 1, 1), 2, depth, pieces))
    anywhere = pl.BlockSpec(memory_space=pl.ANY)
    return pl.pallas_call(
        functools.partial(gather_kernel, depth, width, pieces),
        out_shape=jax.ShapeDtypeStruct((bands,) + own.shape, own.dtype),
        in_specs=[anywhere],
        out_specs=anywhere,
        scratch_shapes=[pltpu.SemaphoreType.DMA, line, line, cross, cross],
        compiler_params=pltpu.CompilerParams(collective_id=0, has_side_effects=True),
    )(own)


def body(coeffs, potential, stick_cells, block, rotation):
    col_count, slots = coeffs.shape[1:]
    planes, size_x, size_y = potential.shape
    groups = lax.axis_size("ga")
    cols = stick_cells.shape[0]
    size_z = planes * groups
    radius = reach(cols, size_x, size_y)
    xw = window(radius, size_x, 16)
    yw = window(radius, size_y, 128)
    slot_ids = slot_index(slots, size_z)
    table_z = hartley(size_z)[:, slot_ids]
    freq_x = signed_freq(stick_cells // size_y, size_x)
    freq_y = signed_freq(stick_cells % size_y, size_y)
    rows = (freq_x + xw // 2) * yw + freq_y + yw // 2

    mine = lax.axis_index("ga") * col_count
    local_x = lax.dynamic_slice_in_dim(freq_x, mine, col_count).astype(F32)
    local_y = lax.dynamic_slice_in_dim(freq_y, mine, col_count).astype(F32)
    plane_part = 0.5 * (
        (2.0 * math.pi / size_x) ** 2 * local_x * local_x
        + (2.0 * math.pi / size_y) ** 2 * local_y * local_y
    )
    freq_z = signed_np(slot_ids, size_z)
    line_part = jnp.asarray(0.5 * (2.0 * math.pi / size_z) ** 2 * freq_z * freq_z, F32)
    kinetic = plane_part[:, None] + line_part[None, :]

    table_f = jnp.asarray(table_z.reshape(groups, planes, slots), F32)
    table_b = jnp.asarray(table_z.reshape(groups, planes, slots), F32)
    high = lax.Precision.HIGH
    sent = jnp.einsum("sk,gzk->gsz", coeffs[0], table_f, precision=high).astype(BF16)
    spread = lax.all_to_all(sent, "ga", split_axis=0, concat_axis=0, tiled=True)
    spread = spread.reshape(cols, planes)
    picked = apply_planes(rows, spread, potential, xw, yw)
    picked = picked.reshape(groups, col_count, planes)
    returned = lax.all_to_all(picked, "ga", split_axis=0, concat_axis=0, tiled=True)
    results = (
        jnp.einsum("gsz,gzk->sk", returned.astype(F32), table_b, precision=high) + (kinetic + LEVEL) * coeffs[0]
    )
    panel = gather_panel(results.astype(BF16), lax.axis_size("band"))
    summed = jnp.dot(
        rotation,
        panel.reshape(panel.shape[0], col_count * slots),
        preferred_element_type=F32,
    )
    rotated = (block.astype(F32) + summed).astype(BF16)
    return (results[None], rotated)


def solution(mesh):
    return jax.shard_map(
        body,
        mesh=mesh,
        in_specs=(
            P("band", "ga", None),
            P("ga", None, None),
            P(),
            P("band", "ga"),
            P("band", None),
        ),
        out_specs=(P("band", "ga", None), P("band", "ga")),
        check_vma=False,
    )
```

```python
import functools
import math

import jax
import jax.numpy as jnp
import numpy as np
from jax import lax
from jax.experimental import pallas as pl
from jax.experimental.pallas import tpu as pltpu
from jax.sharding import PartitionSpec as P

BF16 = jnp.bfloat16
F32 = jnp.float32
LEVEL = -0.5
BATCH = 8


def hartley(count):
    index_row = np.arange(count, dtype=np.int64)
    angles = (index_row[:, None] * index_row[None, :] % count) * (2.0 * math.pi / count)
    return (np.cos(angles) + np.sin(angles)) / math.sqrt(count)


def slot_index(slots, size_z):
    index_row = np.arange(slots)
    return np.where(2 * index_row < slots, index_row, index_row + size_z - slots)


def signed_np(values, count):
    return np.where(2 * values <= count, values, values - count)


def reach(cols, size_x, size_y):
    fx = signed_np(np.arange(size_x), size_x)
    fy = signed_np(np.arange(size_y), size_y)
    radius_sq = np.sort((fx[:, None] ** 2 + fy[None, :] ** 2).reshape(-1))
    return math.isqrt(int(radius_sq[cols - 1]))


def window(radius, size, step):
    return min(size, -(-(2 * radius + 1) // step) * step)


def signed_freq(values, count):
    return jnp.where(2 * values <= count, values, values - count)


def loop(count):
    return lambda step_fn: lax.fori_loop(0, count, step_fn, 0)


def plane_kernel(
    xw, yw, rows_ref, spread_ref, pot_ref, sy_ref, syt_ref, sx_ref, sxt_ref, out_ref, cols_ref, grid_ref, line_ref
):
    planes = pot_ref.shape[0]
    cols = cols_ref.shape[0]
    grid_ref[...] = jnp.zeros_like(grid_ref)
    fold = 128 // planes
    groups, packed = spread_ref.shape[:2]
    spots = [(g, f, (g * fold + f) * packed) for g in range(groups) for f in range(fold)]
    for g, f, base in spots:
        cols_ref[base : base + packed, :planes] = spread_ref[g, :, f * planes : (f + 1) * planes].astype(F32)

    @loop(cols // 32)
    def _(step, carry):
        base = pl.multiple_of(step * 32, 32)
        for i in range(32):
            grid_ref[pl.ds(rows_ref[base + i], 1), :] = cols_ref[pl.ds(base + i, 1), :]
        return carry

    for slot in range(xw):
        chunk = jnp.transpose(grid_ref[slot * yw : (slot + 1) * yw, :])
        for half in range(yw // 128):
            line_ref[half, pl.ds(slot, planes, stride=xw), :] = chunk[:planes, half * 128 : (half + 1) * 128]

    @loop(planes // BATCH)
    def _(step, carry):
        ats = [pl.ds(pl.multiple_of((step * BATCH + i) * xw, xw), xw) for i in range(BATCH)]
        halves = range(yw // 128)
        def join(parts):
            return parts[0] if len(parts) == 1 else jnp.concatenate(parts, axis=1)
        part = jnp.concatenate([join([line_ref[h, at, :].astype(BF16) for h in halves]) for at in ats], axis=0)
        lines = jnp.dot(part, sy_ref[...], preferred_element_type=F32).astype(BF16)
        low = []
        for i in range(BATCH):
            field = jnp.dot(sx_ref[...], lines[i * xw : (i + 1) * xw], preferred_element_type=F32)
            product = (field * (pot_ref[step * BATCH + i].astype(F32) - LEVEL)).astype(BF16)
            low.append(jnp.dot(sxt_ref[...], product, preferred_element_type=F32).astype(BF16))
        back = jnp.dot(jnp.concatenate(low, axis=0), syt_ref[...], preferred_element_type=F32)
        for i, at in enumerate(ats):
            for h in halves:
                line_ref[h, at, :] = back[i * xw : (i + 1) * xw, h * 128 : (h + 1) * 128]
        return carry

    for slot in range(xw):
        parts = [line_ref[half, pl.ds(slot, planes, stride=xw), :] for half in range(yw // 128)]
        chunk = parts[0] if len(parts) == 1 else jnp.concatenate(parts, axis=1)
        if planes < 128:
            chunk = jnp.concatenate([chunk, jnp.zeros((128 - planes, yw), F32)], axis=0)
        grid_ref[slot * yw : (slot + 1) * yw, :] = jnp.transpose(chunk)

    @loop(cols // 32)
    def _(step, carry):
        base = pl.multiple_of(step * 32, 32)
        for i in range(32):
            cols_ref[pl.ds(base + i, 1), :] = grid_ref[pl.ds(rows_ref[base + i], 1), :]
        return carry

    for g in range(groups):
        parts = [cols_ref[base : base + packed, :planes] for at, f, base in spots if at == g]
        out_ref[g] = jnp.concatenate(parts, axis=1).astype(BF16)


def apply_planes(rows, spread, potential, xw, yw):
    planes, size_x, size_y = potential.shape
    cols = rows.shape[0]
    table_x = hartley(size_x)[:, (np.arange(xw) - xw // 2) % size_x]
    table_y = hartley(size_y)[:, (np.arange(yw) - yw // 2) % size_y]
    vmem = pl.BlockSpec(memory_space=pltpu.VMEM)
    cast = lambda a: jnp.asarray(a, BF16)
    return pl.pallas_call(
        functools.partial(plane_kernel, xw, yw),
        out_shape=jax.ShapeDtypeStruct(spread.shape, BF16),
        in_specs=[pl.BlockSpec(memory_space=pltpu.SMEM)] + [vmem] * 6,
        out_specs=vmem,
        scratch_shapes=[
            pltpu.VMEM((cols, 128), F32),
            pltpu.VMEM((xw * yw, 128), F32),
            pltpu.VMEM((yw // 128, planes * xw, 128), F32),
        ],
        compiler_params=pltpu.CompilerParams(vmem_limit_bytes=56 * 2**20),
    )(rows, spread, potential, cast(table_y.T), cast(table_y), cast(table_x), cast(table_x.T))


def peer_hops(groups):
    return sorted(range(1, groups), key=lambda hop: -min(hop, groups - hop))


def spread_kernel(groups, coeffs_ref, table_ref, out_ref, stage_ref, own_sem, send_sem, recv_sem):
    me = lax.axis_index("ga")
    packed = out_ref.shape[1]
    fold = coeffs_ref.shape[0] // packed

    def transform(to):
        table = table_ref[to]
        parts = [
            jnp.dot(coeffs_ref[f * packed : (f + 1) * packed, :].astype(BF16), table, preferred_element_type=F32)
            for f in range(fold)
        ]
        return jnp.concatenate(parts, axis=1).astype(BF16)

    barrier = pltpu.get_barrier_semaphore()
    for hop in peer_hops(groups):
        pl.semaphore_signal(
            barrier,
            inc=1,
            device_id={"ga": (me + hop) % groups},
            device_id_type=pl.DeviceIdType.MESH,
        )
    copies = []
    for place, hop in enumerate(peer_hops(groups)):
        to = (me + hop) % groups
        stage_ref[hop] = transform(to)
        if place == 0:
            pl.semaphore_wait(barrier, groups - 1)
        copy = pltpu.make_async_remote_copy(
            src_ref=stage_ref.at[hop],
            dst_ref=out_ref.at[me],
            send_sem=send_sem.at[hop],
            recv_sem=recv_sem.at[hop],
            device_id={"ga": to},
            device_id_type=pl.DeviceIdType.MESH,
        )
        copy.start()
        copies.append(copy)
    stage_ref[0] = transform(me)
    own = pltpu.make_async_copy(stage_ref.at[0], out_ref.at[me], own_sem)
    own.start()
    own.wait()
    for hop in peer_hops(groups):
        at = out_ref.at[(me + groups - hop) % groups]
        pltpu.make_async_copy(at, at, recv_sem.at[hop]).wait()
    for copy in copies:
        copy.wait_send()


def spread_columns(coeffs, table_z, groups, planes):
    col_count, slots = coeffs.shape
    packed = col_count * planes // 128
    table = table_z.reshape(groups, planes, slots).transpose(0, 2, 1)
    vmem = pl.BlockSpec(memory_space=pltpu.VMEM)
    return pl.pallas_call(
        functools.partial(spread_kernel, groups),
        out_shape=jax.ShapeDtypeStruct((groups, packed, 128), BF16),
        in_specs=[vmem, vmem],
        out_specs=pl.BlockSpec(memory_space=pl.ANY),
        scratch_shapes=[
            pltpu.VMEM((groups, packed, 128), BF16),
            pltpu.SemaphoreType.DMA,
            pltpu.SemaphoreType.DMA((groups,)),
            pltpu.SemaphoreType.DMA((groups,)),
        ],
        compiler_params=pltpu.CompilerParams(
            collective_id=1, has_side_effects=True, vmem_limit_bytes=32 * 2**20
        ),
    )(coeffs, jnp.asarray(table, BF16))


def gather_kernel(
    depth,
    width,
    pieces,
    groups,
    picked_ref,
    coeffs_ref,
    kinetic_ref,
    table_ref,
    h_ref,
    out_ref,
    back_ref,
    own_ref,
    own_sem,
    back_own,
    back_send,
    back_recv,
    line_send,
    line_recv,
    cross_send,
    cross_recv,
):
    band = lax.axis_index("band")
    z = band // width
    x = band % width
    rows = own_ref.shape[0] // pieces
    ways = (1, -1)
    me = lax.axis_index("ga")
    packed = back_ref.shape[1]
    fold = own_ref.shape[0] // packed
    planes = 128 // fold

    def inside(at):
        return jnp.logical_and(at >= 0, at < depth)

    def source(d, slot, cut):
        return own_ref.at[cut, :] if d == 0 else out_ref.at[slot, cut, :]

    def line_copy(way, d, piece):
        cut = pl.ds(piece * rows, rows)
        slot = (z - ways[way] * d) * width + x
        return pltpu.make_async_remote_copy(
            src_ref=source(d, slot, cut),
            dst_ref=out_ref.at[slot, cut, :],
            send_sem=line_send.at[way, d, piece],
            recv_sem=line_recv.at[way, d, piece],
            device_id={"band": (z + ways[way]) * width + x},
            device_id_type=pl.DeviceIdType.MESH,
        )

    def cross_copy(hop, way, d, piece):
        cut = pl.ds(piece * rows, rows)
        slot = (z - ways[way] * d) * width + x
        return pltpu.make_async_remote_copy(
            src_ref=source(d, slot, cut),
            dst_ref=out_ref.at[slot, cut, :],
            send_sem=cross_send.at[hop - 1, way, d, piece],
            recv_sem=cross_recv.at[hop - 1, way, d, piece],
            device_id={"band": z * width + (x + hop) % width},
            device_id_type=pl.DeviceIdType.MESH,
        )

    def line_arrival(way, d, piece):
        cut = pl.ds(piece * rows, rows)
        slot = (z - ways[way] * d) * width + x
        return pltpu.make_async_copy(
            out_ref.at[slot, cut, :], out_ref.at[slot, cut, :], line_recv.at[way, d - 1, piece]
        )

    def cross_arrival(hop, way, d, piece):
        cut = pl.ds(piece * rows, rows)
        slot = (z - ways[way] * d) * width + (x + width - hop) % width
        return pltpu.make_async_copy(
            out_ref.at[slot, cut, :], out_ref.at[slot, cut, :], cross_recv.at[hop - 1, way, d, piece]
        )

    barrier = pltpu.get_barrier_semaphore()
    for way in ways:

        @pl.when(inside(z + way))
        def _(way=way):
            pl.semaphore_signal(
                barrier,
                inc=1,
                device_id={"band": (z + way) * width + x},
                device_id_type=pl.DeviceIdType.MESH,
            )

    for hop in range(1, width):
        pl.semaphore_signal(
            barrier,
            inc=1,
            device_id={"band": z * width + (x + hop) % width},
            device_id_type=pl.DeviceIdType.MESH,
        )
    beside = jnp.where(z > 0, 1, 0) + jnp.where(z < depth - 1, 1, 0)
    for hop in peer_hops(groups):
        pl.semaphore_signal(
            barrier,
            inc=1,
            device_id={"ga": (me + hop) % groups},
            device_id_type=pl.DeviceIdType.MESH,
        )
    pl.semaphore_wait(barrier, beside + width + groups - 2)

    sent = []
    for hop in peer_hops(groups):
        to = (me + hop) % groups
        copy = pltpu.make_async_remote_copy(
            src_ref=picked_ref.at[to],
            dst_ref=back_ref.at[me],
            send_sem=back_send.at[hop],
            recv_sem=back_recv.at[hop],
            device_id={"ga": to},
            device_id_type=pl.DeviceIdType.MESH,
        )
        copy.start()
        sent.append(copy)
    mine = pltpu.make_async_copy(picked_ref.at[me], back_ref.at[me], back_own)
    mine.start()
    mine.wait()
    for hop in peer_hops(groups):
        at = back_ref.at[(me + groups - hop) % groups]
        pltpu.make_async_copy(at, at, back_recv.at[hop]).wait()
    for f in range(fold):
        at = slice(f * packed, (f + 1) * packed)
        lines = jnp.concatenate(
            [back_ref[g, :, f * planes : (f + 1) * planes] for g in range(groups)], axis=1
        )
        total = jnp.dot(lines, table_ref[...], preferred_element_type=F32)
        total = total + kinetic_ref[at, :] * coeffs_ref[at, :]
        h_ref[at, :] = total
        own_ref[at, :] = total.astype(BF16)

    own = pltpu.make_async_copy(own_ref, out_ref.at[band], own_sem)
    own.start()

    for d in range(depth):
        for piece in range(pieces):
            for way in range(2):

                @pl.when(inside(z - ways[way] * d))
                def _(way=way):
                    if d > 0:
                        line_arrival(way, d, piece).wait()

                    if d < depth - 1:

                        @pl.when(inside(z + ways[way]))
                        def _():
                            line_copy(way, d, piece).start()

                    if d > 0 or way == 0:
                        for hop in range(1, width):
                            cross_copy(hop, way, d, piece).start()

    for copy in sent:
        copy.wait_send()
    own.wait()
    for d in range(depth):
        for piece in range(pieces):
            for way in range(2):

                @pl.when(inside(z - ways[way] * d))
                def _(way=way):
                    if d < depth - 1:

                        @pl.when(inside(z + ways[way]))
                        def _():
                            line_copy(way, d, piece).wait_send()

                    if d > 0 or way == 0:
                        for hop in range(1, width):
                            cross_copy(hop, way, d, piece).wait_send()
                            cross_arrival(hop, way, d, piece).wait()


def finish(picked, coeffs, kinetic, table_z, bands):
    groups = picked.shape[0]
    width = bands // 4 if bands % 4 == 0 and bands > 4 else 1
    depth = bands // width
    pieces = 2
    line = pltpu.SemaphoreType.DMA((2, depth, pieces))
    cross = pltpu.SemaphoreType.DMA((max(width - 1, 1), 2, depth, pieces))
    peers = pltpu.SemaphoreType.DMA((groups,))
    one = pltpu.SemaphoreType.DMA
    anywhere = pl.BlockSpec(memory_space=pl.ANY)
    vmem = pl.BlockSpec(memory_space=pltpu.VMEM)
    return pl.pallas_call(
        functools.partial(gather_kernel, depth, width, pieces, groups),
        out_shape=(
            jax.ShapeDtypeStruct(coeffs.shape, F32),
            jax.ShapeDtypeStruct((bands,) + coeffs.shape, BF16),
        ),
        in_specs=[anywhere, vmem, vmem, vmem],
        out_specs=(vmem, anywhere),
        scratch_shapes=[
            pltpu.VMEM(picked.shape, BF16),
            pltpu.VMEM(coeffs.shape, BF16),
        ]
        + [one, one, peers, peers, line, line, cross, cross],
        compiler_params=pltpu.CompilerParams(
            collective_id=0, has_side_effects=True, vmem_limit_bytes=32 * 2**20
        ),
    )(picked, coeffs, kinetic, jnp.asarray(table_z, BF16))


def body(coeffs, potential, stick_cells, block, rotation):
    col_count, slots = coeffs.shape[1:]
    planes, size_x, size_y = potential.shape
    groups = lax.axis_size("ga")
    cols = stick_cells.shape[0]
    size_z = planes * groups
    radius = reach(cols, size_x, size_y)
    xw = window(radius, size_x, 16)
    yw = window(radius, size_y, 128)
    slot_ids = slot_index(slots, size_z)
    table_z = hartley(size_z)[:, slot_ids]
    freq_x = signed_freq(stick_cells // size_y, size_x)
    freq_y = signed_freq(stick_cells % size_y, size_y)
    rows = (freq_x + xw // 2) * yw + freq_y + yw // 2

    mine = lax.axis_index("ga") * col_count
    local_x = lax.dynamic_slice_in_dim(freq_x, mine, col_count).astype(F32)
    local_y = lax.dynamic_slice_in_dim(freq_y, mine, col_count).astype(F32)
    plane_part = 0.5 * (
        (2.0 * math.pi / size_x) ** 2 * local_x * local_x
        + (2.0 * math.pi / size_y) ** 2 * local_y * local_y
    )
    freq_z = signed_np(slot_ids, size_z)
    line_part = jnp.asarray(0.5 * (2.0 * math.pi / size_z) ** 2 * freq_z * freq_z, F32)
    kinetic = plane_part[:, None] + line_part[None, :]

    spread = spread_columns(coeffs[0], table_z, groups, planes)
    picked = apply_planes(rows, spread, potential, xw, yw)
    results, panel = finish(picked, coeffs[0], kinetic + LEVEL, table_z, lax.axis_size("band"))
    summed = jnp.dot(
        rotation,
        panel.reshape(panel.shape[0], col_count * slots),
        preferred_element_type=F32,
    )
    rotated = (block.astype(F32) + summed).astype(BF16)
    return (results[None], rotated)


def solution(mesh):
    return jax.shard_map(
        body,
        mesh=mesh,
        in_specs=(
            P("band", "ga", None),
            P("ga", None, None),
            P(),
            P("band", "ga"),
            P("band", None),
        ),
        out_specs=(P("band", "ga", None), P("band", "ga")),
        check_vma=False,
    )
```

```python
import functools
import math

import jax
import jax.numpy as jnp
import numpy as np
from jax import lax
from jax.experimental import pallas as pl
from jax.experimental.pallas import tpu as pltpu
from jax.sharding import PartitionSpec as P

BF16 = jnp.bfloat16
F32 = jnp.float32
LEVEL = -0.5
BATCH = 16
CUTS = 2


def hartley(count):
    index_row = np.arange(count, dtype=np.int64)
    angles = (index_row[:, None] * index_row[None, :] % count) * (2.0 * math.pi / count)
    return (np.cos(angles) + np.sin(angles)) / math.sqrt(count)


def slot_index(slots, size_z):
    index_row = np.arange(slots)
    return np.where(2 * index_row < slots, index_row, index_row + size_z - slots)


def signed_np(values, count):
    return np.where(2 * values <= count, values, values - count)


def reach(cols, size_x, size_y):
    fx = signed_np(np.arange(size_x), size_x)
    fy = signed_np(np.arange(size_y), size_y)
    radius_sq = np.sort((fx[:, None] ** 2 + fy[None, :] ** 2).reshape(-1))
    return math.isqrt(int(radius_sq[cols - 1]))


def window(radius, size, step):
    return min(size, -(-(2 * radius + 1) // step) * step)


def signed_freq(values, count):
    return jnp.where(2 * values <= count, values, values - count)


def loop(count):
    return lambda step_fn: lax.fori_loop(0, count, step_fn, 0)


def plane_kernel(
    xw, yw, rows_ref, spread_ref, pot_ref, sy_ref, syt_ref, sx_ref, sxt_ref, out_ref, cols_ref, grid_ref, line_ref
):
    planes = pot_ref.shape[0]
    cols = cols_ref.shape[0]
    grid_ref[...] = jnp.zeros_like(grid_ref)
    fold = 128 // planes
    groups, packed = spread_ref.shape[:2]
    part = packed // CUTS
    spots = [
        (g, c, f, ((g * CUTS + c) * fold + f) * part)
        for g in range(groups)
        for c in range(CUTS)
        for f in range(fold)
    ]
    for g, c, f, base in spots:
        held = spread_ref[g, c * part : (c + 1) * part, f * planes : (f + 1) * planes]
        cols_ref[base : base + part, :planes] = held.astype(F32)

    @loop(cols // 32)
    def _(step, carry):
        base = pl.multiple_of(step * 32, 32)
        for i in range(32):
            grid_ref[pl.ds(rows_ref[base + i], 1), :] = cols_ref[pl.ds(base + i, 1), :]
        return carry

    for slot in range(xw):
        chunk = jnp.transpose(grid_ref[slot * yw : (slot + 1) * yw, :])
        for half in range(yw // 128):
            line_ref[half, pl.ds(slot, planes, stride=xw), :] = chunk[:planes, half * 128 : (half + 1) * 128]

    @loop(planes // BATCH)
    def _(step, carry):
        ats = [pl.ds(pl.multiple_of((step * BATCH + i) * xw, xw), xw) for i in range(BATCH)]
        halves = range(yw // 128)
        def join(parts):
            return parts[0] if len(parts) == 1 else jnp.concatenate(parts, axis=1)
        rows_in = jnp.concatenate([join([line_ref[h, at, :].astype(BF16) for h in halves]) for at in ats], axis=0)
        lines = jnp.dot(rows_in, sy_ref[...], preferred_element_type=F32).astype(BF16)
        low = []
        for i in range(BATCH):
            field = jnp.dot(sx_ref[...], lines[i * xw : (i + 1) * xw], preferred_element_type=F32)
            product = (field * (pot_ref[step * BATCH + i].astype(F32) - LEVEL)).astype(BF16)
            low.append(jnp.dot(sxt_ref[...], product, preferred_element_type=F32).astype(BF16))
        back = jnp.dot(jnp.concatenate(low, axis=0), syt_ref[...], preferred_element_type=F32)
        for i, at in enumerate(ats):
            for h in halves:
                line_ref[h, at, :] = back[i * xw : (i + 1) * xw, h * 128 : (h + 1) * 128]
        return carry

    for slot in range(xw):
        parts = [line_ref[half, pl.ds(slot, planes, stride=xw), :] for half in range(yw // 128)]
        chunk = parts[0] if len(parts) == 1 else jnp.concatenate(parts, axis=1)
        if planes < 128:
            chunk = jnp.concatenate([chunk, jnp.zeros((128 - planes, yw), F32)], axis=0)
        grid_ref[slot * yw : (slot + 1) * yw, :] = jnp.transpose(chunk)

    @loop(cols // 32)
    def _(step, carry):
        base = pl.multiple_of(step * 32, 32)
        for i in range(32):
            cols_ref[pl.ds(base + i, 1), :] = grid_ref[pl.ds(rows_ref[base + i], 1), :]
        return carry

    for g in range(groups):
        for c in range(CUTS):
            parts = [cols_ref[base : base + part, :planes] for *at, _, base in spots if at == [g, c]]
            out_ref[g, c * part : (c + 1) * part, :] = jnp.concatenate(parts, axis=1).astype(BF16)


def apply_planes(rows, spread, potential, xw, yw):
    planes, size_x, size_y = potential.shape
    cols = rows.shape[0]
    table_x = hartley(size_x)[:, (np.arange(xw) - xw // 2) % size_x]
    table_y = hartley(size_y)[:, (np.arange(yw) - yw // 2) % size_y]
    vmem = pl.BlockSpec(memory_space=pltpu.VMEM)
    cast = lambda a: jnp.asarray(a, BF16)
    return pl.pallas_call(
        functools.partial(plane_kernel, xw, yw),
        out_shape=jax.ShapeDtypeStruct(spread.shape, BF16),
        in_specs=[pl.BlockSpec(memory_space=pltpu.SMEM)] + [vmem] * 6,
        out_specs=vmem,
        scratch_shapes=[
            pltpu.VMEM((cols, 128), F32),
            pltpu.VMEM((xw * yw, 128), F32),
            pltpu.VMEM((yw // 128, planes * xw, 128), F32),
        ],
        compiler_params=pltpu.CompilerParams(vmem_limit_bytes=56 * 2**20),
    )(rows, spread, potential, cast(table_y.T), cast(table_y), cast(table_x), cast(table_x.T))


def peer_hops(groups):
    return sorted(range(1, groups), key=lambda hop: -min(hop, groups - hop))


def spread_kernel(groups, coeffs_ref, table_ref, out_ref, stage_ref, own_sem, send_sem, recv_sem):
    me = lax.axis_index("ga")
    packed = out_ref.shape[1]
    fold = coeffs_ref.shape[0] // packed

    def transform(to):
        table = table_ref[to]
        part = packed // CUTS
        lines = [
            jnp.dot(coeffs_ref[i * part : (i + 1) * part, :].astype(BF16), table, preferred_element_type=F32)
            for i in range(CUTS * fold)
        ]
        lines = [jnp.concatenate(lines[c * fold : (c + 1) * fold], axis=1) for c in range(CUTS)]
        return jnp.concatenate(lines, axis=0).astype(BF16)

    barrier = pltpu.get_barrier_semaphore()
    for hop in peer_hops(groups):
        pl.semaphore_signal(
            barrier,
            inc=1,
            device_id={"ga": (me + hop) % groups},
            device_id_type=pl.DeviceIdType.MESH,
        )
    copies = []
    for place, hop in enumerate(peer_hops(groups)):
        to = (me + hop) % groups
        stage_ref[hop] = transform(to)
        if place == 0:
            pl.semaphore_wait(barrier, groups - 1)
        copy = pltpu.make_async_remote_copy(
            src_ref=stage_ref.at[hop],
            dst_ref=out_ref.at[me],
            send_sem=send_sem.at[hop],
            recv_sem=recv_sem.at[hop],
            device_id={"ga": to},
            device_id_type=pl.DeviceIdType.MESH,
        )
        copy.start()
        copies.append(copy)
    stage_ref[0] = transform(me)
    own = pltpu.make_async_copy(stage_ref.at[0], out_ref.at[me], own_sem)
    own.start()
    own.wait()
    for hop in peer_hops(groups):
        at = out_ref.at[(me + groups - hop) % groups]
        pltpu.make_async_copy(at, at, recv_sem.at[hop]).wait()
    for copy in copies:
        copy.wait_send()


def spread_columns(coeffs, table_z, groups, planes):
    col_count, slots = coeffs.shape
    packed = col_count * planes // 128
    table = table_z.reshape(groups, planes, slots).transpose(0, 2, 1)
    vmem = pl.BlockSpec(memory_space=pltpu.VMEM)
    return pl.pallas_call(
        functools.partial(spread_kernel, groups),
        out_shape=jax.ShapeDtypeStruct((groups, packed, 128), BF16),
        in_specs=[vmem, vmem],
        out_specs=pl.BlockSpec(memory_space=pl.ANY),
        scratch_shapes=[
            pltpu.VMEM((groups, packed, 128), BF16),
            pltpu.SemaphoreType.DMA,
            pltpu.SemaphoreType.DMA((groups,)),
            pltpu.SemaphoreType.DMA((groups,)),
        ],
        compiler_params=pltpu.CompilerParams(
            collective_id=1, has_side_effects=True, vmem_limit_bytes=32 * 2**20
        ),
    )(coeffs, jnp.asarray(table, BF16))


def gather_kernel(
    depth,
    width,
    pieces,
    groups,
    picked_ref,
    coeffs_ref,
    kinetic_ref,
    table_ref,
    h_ref,
    out_ref,
    back_ref,
    own_ref,
    own_sem,
    back_own,
    back_send,
    back_recv,
    line_send,
    line_recv,
    cross_send,
    cross_recv,
):
    band = lax.axis_index("band")
    z = band // width
    x = band % width
    rows = own_ref.shape[0] // pieces
    ways = (1, -1)
    me = lax.axis_index("ga")
    packed = back_ref.shape[1]
    fold = own_ref.shape[0] // packed
    planes = 128 // fold

    def inside(at):
        return jnp.logical_and(at >= 0, at < depth)

    def source(d, slot, cut):
        return own_ref.at[cut, :] if d == 0 else out_ref.at[slot, cut, :]

    def line_copy(way, d, piece):
        cut = pl.ds(piece * rows, rows)
        slot = (z - ways[way] * d) * width + x
        return pltpu.make_async_remote_copy(
            src_ref=source(d, slot, cut),
            dst_ref=out_ref.at[slot, cut, :],
            send_sem=line_send.at[way, d, piece],
            recv_sem=line_recv.at[way, d, piece],
            device_id={"band": (z + ways[way]) * width + x},
            device_id_type=pl.DeviceIdType.MESH,
        )

    def cross_copy(hop, way, d, piece):
        cut = pl.ds(piece * rows, rows)
        slot = (z - ways[way] * d) * width + x
        return pltpu.make_async_remote_copy(
            src_ref=source(d, slot, cut),
            dst_ref=out_ref.at[slot, cut, :],
            send_sem=cross_send.at[hop - 1, way, d, piece],
            recv_sem=cross_recv.at[hop - 1, way, d, piece],
            device_id={"band": z * width + (x + hop) % width},
            device_id_type=pl.DeviceIdType.MESH,
        )

    def line_arrival(way, d, piece):
        cut = pl.ds(piece * rows, rows)
        slot = (z - ways[way] * d) * width + x
        return pltpu.make_async_copy(
            out_ref.at[slot, cut, :], out_ref.at[slot, cut, :], line_recv.at[way, d - 1, piece]
        )

    def cross_arrival(hop, way, d, piece):
        cut = pl.ds(piece * rows, rows)
        slot = (z - ways[way] * d) * width + (x + width - hop) % width
        return pltpu.make_async_copy(
            out_ref.at[slot, cut, :], out_ref.at[slot, cut, :], cross_recv.at[hop - 1, way, d, piece]
        )

    def pass_on(d, piece):
        for way in range(2):

            @pl.when(inside(z - ways[way] * d))
            def _(way=way):
                if d > 0:
                    line_arrival(way, d, piece).wait()

                if d < depth - 1:

                    @pl.when(inside(z + ways[way]))
                    def _():
                        line_copy(way, d, piece).start()

                if d > 0 or way == 0:
                    for hop in range(1, width):
                        cross_copy(hop, way, d, piece).start()

    barrier = pltpu.get_barrier_semaphore()
    for way in ways:

        @pl.when(inside(z + way))
        def _(way=way):
            pl.semaphore_signal(
                barrier,
                inc=1,
                device_id={"band": (z + way) * width + x},
                device_id_type=pl.DeviceIdType.MESH,
            )

    for hop in range(1, width):
        pl.semaphore_signal(
            barrier,
            inc=1,
            device_id={"band": z * width + (x + hop) % width},
            device_id_type=pl.DeviceIdType.MESH,
        )
    beside = jnp.where(z > 0, 1, 0) + jnp.where(z < depth - 1, 1, 0)
    for hop in peer_hops(groups):
        pl.semaphore_signal(
            barrier,
            inc=1,
            device_id={"ga": (me + hop) % groups},
            device_id_type=pl.DeviceIdType.MESH,
        )
    pl.semaphore_wait(barrier, beside + width + groups - 2)

    part = packed // CUTS
    sent = []
    for c in range(CUTS):
        cut = pl.ds(c * part, part)
        for hop in peer_hops(groups):
            to = (me + hop) % groups
            copy = pltpu.make_async_remote_copy(
                src_ref=picked_ref.at[to, cut, :],
                dst_ref=back_ref.at[me, cut, :],
                send_sem=back_send.at[hop, c],
                recv_sem=back_recv.at[hop, c],
                device_id={"ga": to},
                device_id_type=pl.DeviceIdType.MESH,
            )
            copy.start()
            sent.append(copy)
    mine = pltpu.make_async_copy(picked_ref.at[me], back_ref.at[me], back_own)
    mine.start()
    mine.wait()
    for c in range(CUTS):
        for hop in peer_hops(groups):
            at = back_ref.at[(me + groups - hop) % groups, pl.ds(c * part, part), :]
            pltpu.make_async_copy(at, at, back_recv.at[hop, c]).wait()
        for f in range(fold):
            at = slice((c * fold + f) * part, (c * fold + f + 1) * part)
            held = slice(c * part, (c + 1) * part)
            lines = jnp.concatenate(
                [back_ref[g, held, f * planes : (f + 1) * planes] for g in range(groups)], axis=1
            )
            total = jnp.dot(lines, table_ref[...], preferred_element_type=F32)
            total = total + kinetic_ref[at, :] * coeffs_ref[at, :]
            h_ref[at, :] = total
            own_ref[at, :] = total.astype(BF16)
        for piece in range(c * pieces // CUTS, (c + 1) * pieces // CUTS):
            pass_on(0, piece)
    own = pltpu.make_async_copy(own_ref, out_ref.at[band], own_sem)
    own.start()

    for d in range(1, depth):
        for piece in range(pieces):
            pass_on(d, piece)

    for copy in sent:
        copy.wait_send()
    own.wait()
    for d in range(depth):
        for piece in range(pieces):
            for way in range(2):

                @pl.when(inside(z - ways[way] * d))
                def _(way=way):
                    if d < depth - 1:

                        @pl.when(inside(z + ways[way]))
                        def _():
                            line_copy(way, d, piece).wait_send()

                    if d > 0 or way == 0:
                        for hop in range(1, width):
                            cross_copy(hop, way, d, piece).wait_send()
                            cross_arrival(hop, way, d, piece).wait()


def finish(picked, coeffs, kinetic, table_z, bands):
    groups = picked.shape[0]
    width = bands // 4 if bands % 4 == 0 and bands > 4 else 1
    depth = bands // width
    pieces = 2 * CUTS
    line = pltpu.SemaphoreType.DMA((2, depth, pieces))
    cross = pltpu.SemaphoreType.DMA((max(width - 1, 1), 2, depth, pieces))
    peers = pltpu.SemaphoreType.DMA((groups, CUTS))
    one = pltpu.SemaphoreType.DMA
    anywhere = pl.BlockSpec(memory_space=pl.ANY)
    vmem = pl.BlockSpec(memory_space=pltpu.VMEM)
    return pl.pallas_call(
        functools.partial(gather_kernel, depth, width, pieces, groups),
        out_shape=(
            jax.ShapeDtypeStruct(coeffs.shape, F32),
            jax.ShapeDtypeStruct((bands,) + coeffs.shape, BF16),
        ),
        in_specs=[anywhere, vmem, vmem, vmem],
        out_specs=(vmem, anywhere),
        scratch_shapes=[
            pltpu.VMEM(picked.shape, BF16),
            pltpu.VMEM(coeffs.shape, BF16),
        ]
        + [one, one, peers, peers, line, line, cross, cross],
        compiler_params=pltpu.CompilerParams(
            collective_id=0, has_side_effects=True, vmem_limit_bytes=32 * 2**20
        ),
    )(picked, coeffs, kinetic, jnp.asarray(table_z, BF16))


def body(coeffs, potential, stick_cells, block, rotation):
    col_count, slots = coeffs.shape[1:]
    planes, size_x, size_y = potential.shape
    groups = lax.axis_size("ga")
    cols = stick_cells.shape[0]
    size_z = planes * groups
    radius = reach(cols, size_x, size_y)
    xw = window(radius, size_x, 16)
    yw = window(radius, size_y, 128)
    slot_ids = slot_index(slots, size_z)
    table_z = hartley(size_z)[:, slot_ids]
    freq_x = signed_freq(stick_cells // size_y, size_x)
    freq_y = signed_freq(stick_cells % size_y, size_y)
    rows = (freq_x + xw // 2) * yw + freq_y + yw // 2

    mine = lax.axis_index("ga") * col_count
    local_x = lax.dynamic_slice_in_dim(freq_x, mine, col_count).astype(F32)
    local_y = lax.dynamic_slice_in_dim(freq_y, mine, col_count).astype(F32)
    plane_part = 0.5 * (
        (2.0 * math.pi / size_x) ** 2 * local_x * local_x
        + (2.0 * math.pi / size_y) ** 2 * local_y * local_y
    )
    freq_z = signed_np(slot_ids, size_z)
    line_part = jnp.asarray(0.5 * (2.0 * math.pi / size_z) ** 2 * freq_z * freq_z, F32)
    kinetic = plane_part[:, None] + line_part[None, :]

    spread = spread_columns(coeffs[0], table_z, groups, planes)
    picked = apply_planes(rows, spread, potential, xw, yw)
    results, panel = finish(picked, coeffs[0], kinetic + LEVEL, table_z, lax.axis_size("band"))
    summed = jnp.dot(
        rotation,
        panel.reshape(panel.shape[0], col_count * slots),
        preferred_element_type=F32,
    )
    rotated = (block.astype(F32) + summed).astype(BF16)
    return (results[None], rotated)


def solution(mesh):
    return jax.shard_map(
        body,
        mesh=mesh,
        in_specs=(
            P("band", "ga", None),
            P("ga", None, None),
            P(),
            P("band", "ga"),
            P("band", None),
        ),
        out_specs=(P("band", "ga", None), P("band", "ga")),
        check_vma=False,
    )
```

```python
import functools
import math

import jax
import jax.numpy as jnp
import numpy as np
from jax import lax
from jax.experimental import pallas as pl
from jax.experimental.pallas import tpu as pltpu
from jax.sharding import PartitionSpec as P

BF16 = jnp.bfloat16
F32 = jnp.float32
LEVEL = -0.5
BATCH = 16
CUTS = 2


def hartley(count):
    index_row = np.arange(count, dtype=np.int64)
    angles = (index_row[:, None] * index_row[None, :] % count) * (2.0 * math.pi / count)
    return (np.cos(angles) + np.sin(angles)) / math.sqrt(count)


def slot_index(slots, size_z):
    index_row = np.arange(slots)
    return np.where(2 * index_row < slots, index_row, index_row + size_z - slots)


def signed_np(values, count):
    return np.where(2 * values <= count, values, values - count)


def reach(cols, size_x, size_y):
    fx = signed_np(np.arange(size_x), size_x)
    fy = signed_np(np.arange(size_y), size_y)
    radius_sq = np.sort((fx[:, None] ** 2 + fy[None, :] ** 2).reshape(-1))
    return math.isqrt(int(radius_sq[cols - 1]))


def window(radius, size, step):
    return min(size, -(-(2 * radius + 1) // step) * step)


def signed_freq(values, count):
    return jnp.where(2 * values <= count, values, values - count)


def loop(count):
    return lambda step_fn: lax.fori_loop(0, count, step_fn, 0)


def plane_kernel(
    xw, yw, rows_ref, spread_ref, pot_ref, sy_ref, syt_ref, sx_ref, sxt_ref, out_ref, cols_ref, grid_ref, line_ref
):
    planes = pot_ref.shape[0]
    cols = cols_ref.shape[0]
    grid_ref[...] = jnp.zeros_like(grid_ref)
    fold = 128 // planes
    groups, packed = spread_ref.shape[:2]
    part = packed // CUTS
    spots = [
        (g, c, f, ((g * CUTS + c) * fold + f) * part)
        for g in range(groups)
        for c in range(CUTS)
        for f in range(fold)
    ]
    for g, c, f, base in spots:
        held = spread_ref[g, c * part : (c + 1) * part, f * planes : (f + 1) * planes]
        cols_ref[base : base + part, :planes] = held.astype(F32)

    @loop(cols // 32)
    def _(step, carry):
        base = pl.multiple_of(step * 32, 32)
        for i in range(32):
            grid_ref[pl.ds(rows_ref[base + i], 1), :] = cols_ref[pl.ds(base + i, 1), :]
        return carry

    for slot in range(xw):
        chunk = jnp.transpose(grid_ref[slot * yw : (slot + 1) * yw, :])
        for half in range(yw // 128):
            line_ref[half, pl.ds(slot, planes, stride=xw), :] = chunk[:planes, half * 128 : (half + 1) * 128]

    @loop(planes // BATCH)
    def _(step, carry):
        ats = [pl.ds(pl.multiple_of((step * BATCH + i) * xw, xw), xw) for i in range(BATCH)]
        halves = range(yw // 128)
        def join(parts):
            return parts[0] if len(parts) == 1 else jnp.concatenate(parts, axis=1)
        rows_in = jnp.concatenate([join([line_ref[h, at, :].astype(BF16) for h in halves]) for at in ats], axis=0)
        lines = jnp.dot(rows_in, sy_ref[...], preferred_element_type=F32).astype(BF16)
        low = []
        for i in range(BATCH):
            field = jnp.dot(sx_ref[...], lines[i * xw : (i + 1) * xw], preferred_element_type=F32)
            product = (field * (pot_ref[step * BATCH + i].astype(F32) - LEVEL)).astype(BF16)
            low.append(jnp.dot(sxt_ref[...], product, preferred_element_type=F32).astype(BF16))
        back = jnp.dot(jnp.concatenate(low, axis=0), syt_ref[...], preferred_element_type=F32)
        for i, at in enumerate(ats):
            for h in halves:
                line_ref[h, at, :] = back[i * xw : (i + 1) * xw, h * 128 : (h + 1) * 128]
        return carry

    for slot in range(xw):
        parts = [line_ref[half, pl.ds(slot, planes, stride=xw), :] for half in range(yw // 128)]
        chunk = parts[0] if len(parts) == 1 else jnp.concatenate(parts, axis=1)
        if planes < 128:
            chunk = jnp.concatenate([chunk, jnp.zeros((128 - planes, yw), F32)], axis=0)
        grid_ref[slot * yw : (slot + 1) * yw, :] = jnp.transpose(chunk)

    @loop(cols // 32)
    def _(step, carry):
        base = pl.multiple_of(step * 32, 32)
        for i in range(32):
            cols_ref[pl.ds(base + i, 1), :] = grid_ref[pl.ds(rows_ref[base + i], 1), :]
        return carry

    for g in range(groups):
        for c in range(CUTS):
            parts = [cols_ref[base : base + part, :planes] for *at, _, base in spots if at == [g, c]]
            out_ref[g, c * part : (c + 1) * part, :] = jnp.concatenate(parts, axis=1).astype(BF16)


def apply_planes(rows, spread, potential, xw, yw):
    planes, size_x, size_y = potential.shape
    cols = rows.shape[0]
    table_x = hartley(size_x)[:, (np.arange(xw) - xw // 2) % size_x]
    table_y = hartley(size_y)[:, (np.arange(yw) - yw // 2) % size_y]
    vmem = pl.BlockSpec(memory_space=pltpu.VMEM)
    cast = lambda a: jnp.asarray(a, BF16)
    return pl.pallas_call(
        functools.partial(plane_kernel, xw, yw),
        out_shape=jax.ShapeDtypeStruct(spread.shape, BF16),
        in_specs=[pl.BlockSpec(memory_space=pltpu.SMEM)] + [vmem] * 6,
        out_specs=vmem,
        scratch_shapes=[
            pltpu.VMEM((cols, 128), F32),
            pltpu.VMEM((xw * yw, 128), F32),
            pltpu.VMEM((yw // 128, planes * xw, 128), F32),
        ],
        compiler_params=pltpu.CompilerParams(vmem_limit_bytes=56 * 2**20),
    )(rows, spread, potential, cast(table_y.T), cast(table_y), cast(table_x), cast(table_x.T))


def peer_hops(groups):
    return sorted(range(1, groups), key=lambda hop: -min(hop, groups - hop))


def spread_kernel(groups, coeffs_ref, table_ref, out_ref, stage_ref, own_sem, send_sem, recv_sem):
    me = lax.axis_index("ga")
    packed = out_ref.shape[1]
    fold = coeffs_ref.shape[0] // packed

    def transform(to):
        table = table_ref[to]
        part = packed // CUTS
        lines = [
            jnp.dot(coeffs_ref[i * part : (i + 1) * part, :].astype(BF16), table, preferred_element_type=F32)
            for i in range(CUTS * fold)
        ]
        lines = [jnp.concatenate(lines[c * fold : (c + 1) * fold], axis=1) for c in range(CUTS)]
        return jnp.concatenate(lines, axis=0).astype(BF16)

    barrier = pltpu.get_barrier_semaphore()
    for hop in peer_hops(groups):
        pl.semaphore_signal(
            barrier,
            inc=1,
            device_id={"ga": (me + hop) % groups},
            device_id_type=pl.DeviceIdType.MESH,
        )
    copies = []
    for place, hop in enumerate(peer_hops(groups)):
        to = (me + hop) % groups
        stage_ref[hop] = transform(to)
        if place == 0:
            pl.semaphore_wait(barrier, groups - 1)
        copy = pltpu.make_async_remote_copy(
            src_ref=stage_ref.at[hop],
            dst_ref=out_ref.at[me],
            send_sem=send_sem.at[hop],
            recv_sem=recv_sem.at[hop],
            device_id={"ga": to},
            device_id_type=pl.DeviceIdType.MESH,
        )
        copy.start()
        copies.append(copy)
    stage_ref[0] = transform(me)
    own = pltpu.make_async_copy(stage_ref.at[0], out_ref.at[me], own_sem)
    own.start()
    own.wait()
    for hop in peer_hops(groups):
        at = out_ref.at[(me + groups - hop) % groups]
        pltpu.make_async_copy(at, at, recv_sem.at[hop]).wait()
    for copy in copies:
        copy.wait_send()


def spread_columns(coeffs, table_z, groups, planes):
    col_count, slots = coeffs.shape
    packed = col_count * planes // 128
    table = table_z.reshape(groups, planes, slots).transpose(0, 2, 1)
    vmem = pl.BlockSpec(memory_space=pltpu.VMEM)
    return pl.pallas_call(
        functools.partial(spread_kernel, groups),
        out_shape=jax.ShapeDtypeStruct((groups, packed, 128), BF16),
        in_specs=[vmem, vmem],
        out_specs=pl.BlockSpec(memory_space=pl.ANY),
        scratch_shapes=[
            pltpu.VMEM((groups, packed, 128), BF16),
            pltpu.SemaphoreType.DMA,
            pltpu.SemaphoreType.DMA((groups,)),
            pltpu.SemaphoreType.DMA((groups,)),
        ],
        compiler_params=pltpu.CompilerParams(
            collective_id=1, has_side_effects=True, vmem_limit_bytes=32 * 2**20
        ),
    )(coeffs, jnp.asarray(table, BF16))


def gather_kernel(
    depth,
    width,
    pieces,
    groups,
    picked_ref,
    coeffs_ref,
    kinetic_ref,
    table_ref,
    h_ref,
    out_ref,
    back_ref,
    own_ref,
    own_sem,
    back_own,
    back_send,
    back_recv,
    line_send,
    line_recv,
    cross_send,
    cross_recv,
):
    band = lax.axis_index("band")
    z = band // width
    x = band % width
    rows = own_ref.shape[0] // pieces
    ways = (1, -1)
    me = lax.axis_index("ga")
    packed = back_ref.shape[1]
    fold = own_ref.shape[0] // packed
    planes = 128 // fold

    def inside(at):
        return jnp.logical_and(at >= 0, at < depth)

    def source(d, slot, cut):
        return own_ref.at[cut, :] if d == 0 else out_ref.at[slot, cut, :]

    def line_copy(way, d, piece):
        cut = pl.ds(piece * rows, rows)
        slot = (z - ways[way] * d) * width + x
        return pltpu.make_async_remote_copy(
            src_ref=source(d, slot, cut),
            dst_ref=out_ref.at[slot, cut, :],
            send_sem=line_send.at[way, d, piece],
            recv_sem=line_recv.at[way, d, piece],
            device_id={"band": (z + ways[way]) * width + x},
            device_id_type=pl.DeviceIdType.MESH,
        )

    def cross_copy(hop, way, d, piece):
        cut = pl.ds(piece * rows, rows)
        slot = (z - ways[way] * d) * width + x
        return pltpu.make_async_remote_copy(
            src_ref=source(d, slot, cut),
            dst_ref=out_ref.at[slot, cut, :],
            send_sem=cross_send.at[hop - 1, way, d, piece],
            recv_sem=cross_recv.at[hop - 1, way, d, piece],
            device_id={"band": z * width + (x + hop) % width},
            device_id_type=pl.DeviceIdType.MESH,
        )

    def line_arrival(way, d, piece):
        cut = pl.ds(piece * rows, rows)
        slot = (z - ways[way] * d) * width + x
        return pltpu.make_async_copy(
            out_ref.at[slot, cut, :], out_ref.at[slot, cut, :], line_recv.at[way, d - 1, piece]
        )

    def cross_arrival(hop, way, d, piece):
        cut = pl.ds(piece * rows, rows)
        slot = (z - ways[way] * d) * width + (x + width - hop) % width
        return pltpu.make_async_copy(
            out_ref.at[slot, cut, :], out_ref.at[slot, cut, :], cross_recv.at[hop - 1, way, d, piece]
        )

    def pass_on(d, piece):
        for way in range(2):

            @pl.when(inside(z - ways[way] * d))
            def _(way=way):
                if d > 0:
                    line_arrival(way, d, piece).wait()

                if d > 0 or way == 0:
                    for hop in range(1, width):
                        cross_copy(hop, way, d, piece).start()

                if d < depth - 1:

                    @pl.when(inside(z + ways[way]))
                    def _():
                        line_copy(way, d, piece).start()

    barrier = pltpu.get_barrier_semaphore()
    for way in ways:

        @pl.when(inside(z + way))
        def _(way=way):
            pl.semaphore_signal(
                barrier,
                inc=1,
                device_id={"band": (z + way) * width + x},
                device_id_type=pl.DeviceIdType.MESH,
            )

    for hop in range(1, width):
        pl.semaphore_signal(
            barrier,
            inc=1,
            device_id={"band": z * width + (x + hop) % width},
            device_id_type=pl.DeviceIdType.MESH,
        )
    beside = jnp.where(z > 0, 1, 0) + jnp.where(z < depth - 1, 1, 0)
    for hop in peer_hops(groups):
        pl.semaphore_signal(
            barrier,
            inc=1,
            device_id={"ga": (me + hop) % groups},
            device_id_type=pl.DeviceIdType.MESH,
        )
    pl.semaphore_wait(barrier, beside + width + groups - 2)

    part = packed // CUTS
    sent = []
    for c in range(CUTS):
        cut = pl.ds(c * part, part)
        for hop in peer_hops(groups):
            to = (me + hop) % groups
            copy = pltpu.make_async_remote_copy(
                src_ref=picked_ref.at[to, cut, :],
                dst_ref=back_ref.at[me, cut, :],
                send_sem=back_send.at[hop, c],
                recv_sem=back_recv.at[hop, c],
                device_id={"ga": to},
                device_id_type=pl.DeviceIdType.MESH,
            )
            copy.start()
            sent.append(copy)
    mine = pltpu.make_async_copy(picked_ref.at[me], back_ref.at[me], back_own)
    mine.start()
    mine.wait()
    for c in range(CUTS):
        for hop in peer_hops(groups):
            at = back_ref.at[(me + groups - hop) % groups, pl.ds(c * part, part), :]
            pltpu.make_async_copy(at, at, back_recv.at[hop, c]).wait()
        for f in range(fold):
            at = slice((c * fold + f) * part, (c * fold + f + 1) * part)
            held = slice(c * part, (c + 1) * part)
            lines = jnp.concatenate(
                [back_ref[g, held, f * planes : (f + 1) * planes] for g in range(groups)], axis=1
            )
            total = jnp.dot(lines, table_ref[...], preferred_element_type=F32)
            total = total + kinetic_ref[at, :] * coeffs_ref[at, :]
            h_ref[at, :] = total
            own_ref[at, :] = total.astype(BF16)
        for piece in range(c * pieces // CUTS, (c + 1) * pieces // CUTS):
            pass_on(0, piece)
    own = pltpu.make_async_copy(own_ref, out_ref.at[band], own_sem)
    own.start()

    for d in range(1, depth):
        for piece in range(pieces):
            pass_on(d, piece)

    for copy in sent:
        copy.wait_send()
    own.wait()
    for d in range(depth):
        for piece in range(pieces):
            for way in range(2):

                @pl.when(inside(z - ways[way] * d))
                def _(way=way):
                    if d < depth - 1:

                        @pl.when(inside(z + ways[way]))
                        def _():
                            line_copy(way, d, piece).wait_send()

                    if d > 0 or way == 0:
                        for hop in range(1, width):
                            cross_copy(hop, way, d, piece).wait_send()
                            cross_arrival(hop, way, d, piece).wait()


def finish(picked, coeffs, kinetic, table_z, bands):
    groups = picked.shape[0]
    width = bands // 4 if bands % 4 == 0 and bands > 4 else 1
    depth = bands // width
    pieces = 2 * CUTS
    line = pltpu.SemaphoreType.DMA((2, depth, pieces))
    cross = pltpu.SemaphoreType.DMA((max(width - 1, 1), 2, depth, pieces))
    peers = pltpu.SemaphoreType.DMA((groups, CUTS))
    one = pltpu.SemaphoreType.DMA
    anywhere = pl.BlockSpec(memory_space=pl.ANY)
    vmem = pl.BlockSpec(memory_space=pltpu.VMEM)
    return pl.pallas_call(
        functools.partial(gather_kernel, depth, width, pieces, groups),
        out_shape=(
            jax.ShapeDtypeStruct(coeffs.shape, F32),
            jax.ShapeDtypeStruct((bands,) + coeffs.shape, BF16),
        ),
        in_specs=[anywhere, vmem, vmem, vmem],
        out_specs=(vmem, anywhere),
        scratch_shapes=[
            pltpu.VMEM(picked.shape, BF16),
            pltpu.VMEM(coeffs.shape, BF16),
        ]
        + [one, one, peers, peers, line, line, cross, cross],
        compiler_params=pltpu.CompilerParams(
            collective_id=0, has_side_effects=True, vmem_limit_bytes=32 * 2**20
        ),
    )(picked, coeffs, kinetic, jnp.asarray(table_z, BF16))


def body(coeffs, potential, stick_cells, block, rotation):
    col_count, slots = coeffs.shape[1:]
    planes, size_x, size_y = potential.shape
    groups = lax.axis_size("ga")
    cols = stick_cells.shape[0]
    size_z = planes * groups
    radius = reach(cols, size_x, size_y)
    xw = window(radius, size_x, 16)
    yw = window(radius, size_y, 128)
    slot_ids = slot_index(slots, size_z)
    table_z = hartley(size_z)[:, slot_ids]
    freq_x = signed_freq(stick_cells // size_y, size_x)
    freq_y = signed_freq(stick_cells % size_y, size_y)
    rows = (freq_x + xw // 2) * yw + freq_y + yw // 2

    mine = lax.axis_index("ga") * col_count
    local_x = lax.dynamic_slice_in_dim(freq_x, mine, col_count).astype(F32)
    local_y = lax.dynamic_slice_in_dim(freq_y, mine, col_count).astype(F32)
    plane_part = 0.5 * (
        (2.0 * math.pi / size_x) ** 2 * local_x * local_x
        + (2.0 * math.pi / size_y) ** 2 * local_y * local_y
    )
    freq_z = signed_np(slot_ids, size_z)
    line_part = jnp.asarray(0.5 * (2.0 * math.pi / size_z) ** 2 * freq_z * freq_z, F32)
    kinetic = plane_part[:, None] + line_part[None, :]

    spread = spread_columns(coeffs[0], table_z, groups, planes)
    picked = apply_planes(rows, spread, potential, xw, yw)
    results, panel = finish(picked, coeffs[0], kinetic + LEVEL, table_z, lax.axis_size("band"))
    summed = jnp.dot(
        rotation,
        panel.reshape(panel.shape[0], col_count * slots),
        preferred_element_type=F32,
    )
    rotated = (block.astype(F32) + summed).astype(BF16)
    return (results[None], rotated)


def solution(mesh):
    return jax.shard_map(
        body,
        mesh=mesh,
        in_specs=(
            P("band", "ga", None),
            P("ga", None, None),
            P(),
            P("band", "ga"),
            P("band", None),
        ),
        out_specs=(P("band", "ga", None), P("band", "ga")),
        check_vma=False,
    )
```
